256 devices in a mesh: row: 4 (over y), col: 8 (over z), depth: 8 (over x, core).
Axes of the slice: x: 4, y: 4, z: 8, core: 2. Of those that a mesh axis runs over, the one named last changes fastest.
Arguments:
- inputs: bfloat16 [512, 12288], P(('row', 'depth'), 'col'), may hold values from -6 to 6
- w_in: bfloat16 [12288, 24576], P('col', ('row', 'depth')), may hold values from -0.0546875 to 0.0546875
- w_out: bfloat16 [24576, 12288], P(('row', 'depth'), 'col'), may hold values from -0.0390625 to 0.0390625
- grad_out: bfloat16 [512, 12288], P(('row', 'depth'), 'col'), may hold values from -6 to 6
Outputs:
- outputs: bfloat16 [512, 12288], P(('row', 'depth'), 'col')
- grad_in: bfloat16 [512, 12288], P(('row', 'depth'), 'col')
- grad_w_in: bfloat16 [12288, 24576], P('col', ('row', 'depth'))
- grad_w_out: bfloat16 [24576, 12288], P(('row', 'depth'), 'col')
The draws below stay inside these ranges and needn't reach their ends.
All inputs are finite; a program needn't handle non-finite values.
Results may differ from the reference program's by a relative error of at most 0.005.
Values may be sent and summed in bfloat16 or wider, within the bound.
A program may use at most 64 MiB of HBM per device.

```python
import jax
import jax.numpy as jnp
from jax import lax

D = 12288
FF = 24576
TOKENS = 512


def block_scale(stream_key, extent, pieces, low, high):
    loudness, own = 1.0, jax.random.fold_in(stream_key, 6)
    for dim, blocks in pieces:
        heights = jnp.exp(jax.random.uniform(jax.random.fold_in(own, dim), (blocks,), jnp.float32, low / len(pieces), high / len(pieces)))
        loudness = loudness * jnp.repeat(heights, extent[dim] // blocks).reshape([-1 if axis == dim else 1 for axis in range(len(extent))])
    return loudness


def scatter_about(own_key, extent, width, limit, pieces=(), held_as=jnp.bfloat16):
    array = jax.random.normal(own_key, extent, jnp.float32) * width
    if len(pieces) > 0:
        array = block_scale(own_key, extent, pieces, -0.22, 0.18) * array
    return jnp.clip(array, min=-limit, max=limit).astype(held_as)


def setup_inputs(seed: int = 0) -> dict:
    key_list = jax.random.split(jax.random.key(seed), 5)
    return {
        "inputs": scatter_about(key_list[0], (TOKENS, D), 1.0, 6.0, ((0, 32), (1, 8))),
        "w_in": scatter_about(key_list[1], (D, FF), D ** -0.5, 0.0546875, ((0, 8), (1, 32))),
        "w_out": scatter_about(key_list[2], (FF, D), FF ** -0.5, 0.0390625, ((0, 32), (1, 8))),
        "grad_out": scatter_about(key_list[3], (TOKENS, D), 1.0, 6.0, ((0, 32), (1, 8))),
    }


def gelu_parts(hidden):
    inner = 0.7978845608 * (hidden + 0.044715 * hidden * hidden * hidden)
    tangent = jnp.tanh(inner)
    value = 0.5 * hidden * (1.0 + tangent)
    slope = 0.5 * (1.0 + tangent) + 0.5 * hidden * (1.0 - tangent * tangent) * 0.7978845608 * (1.0 + 3.0 * 0.044715 * hidden * hidden)
    return value, slope


def contract(left, right, left_dim, right_dim):
    return lax.dot_general(left, right, (((left_dim,), (right_dim,)), ((), ())), preferred_element_type=jnp.float32)


def reference(inputs, w_in, w_out, grad_out):
    factor = 1.0 / (TOKENS ** 0.5)
    hidden = contract(inputs, w_in, 1, 0)
    value, slope = gelu_parts(hidden)
    act = value.astype(jnp.bfloat16)
    outputs = contract(act, w_out, 1, 0).astype(jnp.bfloat16)
    grad_act = contract(grad_out, w_out, 1, 1)
    grad_hidden = (grad_act * slope).astype(jnp.bfloat16)
    grad_in = contract(grad_hidden, w_in, 1, 1).astype(jnp.bfloat16)
    grad_w_in = (contract(inputs, grad_hidden, 0, 0) * factor).astype(jnp.bfloat16)
    grad_w_out = (contract(act, grad_out, 0, 0) * factor).astype(jnp.bfloat16)
    return (outputs, grad_in, grad_w_in, grad_w_out)
```

```python
import functools

import jax
import jax.numpy as jnp
from jax import lax
from jax.experimental import pallas as pl
from jax.experimental.pallas import tpu as pltpu
from jax.sharding import PartitionSpec as P

MESH = pl.DeviceIdType.MESH
BF = jnp.bfloat16
F32 = jnp.float32


def gelu_parts(hidden):
    inner = 0.7978845608 * (hidden + 0.044715 * hidden * hidden * hidden)
    tangent = jnp.tanh(inner)
    value = 0.5 * hidden * (1.0 + tangent)
    slope = 0.5 * (1.0 + tangent) + 0.5 * hidden * (1.0 - tangent * tangent) * 0.7978845608 * (
        1.0 + 3.0 * 0.044715 * hidden * hidden
    )
    return (value, slope)


def contract(left, right, left_dim, right_dim):
    return lax.dot_general(
        left, right, (((left_dim,), (right_dim,)), ((), ())), preferred_element_type=F32
    )


def body(
    n, nz, factor,
    x_hbm, win_hbm, wout_hbm, g_hbm,
    out_ref, gin_ref, gwin_hbm, gwout_hbm,
    acts, win, wout, part, z_send, z_recv, slope_ref, wide,
    own_sum, oth_sum, sib_sum, p1_send, p1_recv, p2_send, p2_recv, fin_send, fin_recv,
    gw_in, gw_out,
    w_sem, gw_sem,
    s1_ssem, s1_rsem, s2_ssem, s2_rsem, sp_ssem, sp_rsem,
    z_ssem, z_rsem, a_ssem, a_rsem,
    sib_ssem, sib_rsem, p1_ssem, p1_rsem, p2_ssem, p2_rsem, fin_ssem, fin_rsem,
):
    y = lax.axis_index("row")
    z = lax.axis_index("col")
    depth = lax.axis_index("depth")
    x, c = depth // 2, lax.rem(depth, 2)
    o = 1 - c
    half = win.shape[1]
    mid = half // 2
    width = win.shape[2]
    wmid = width // 2

    def at(xx, yy, zz, cc):
        return (lax.rem(yy, n), lax.rem(zz, nz), lax.rem(xx, n) * 2 + cc)

    sibling = at(x, y, z, o)
    right, left = at(x, y, z + 1, c), at(x, y, z + nz - 1, c)

    def line1(d):
        return at(x + d * o, y + d * c, z, c)

    def line2(d):
        return at(x + d * c, y + d * o, z, c)

    q1, q2 = x * o + y * c, y * o + x * c
    r1, r2 = q2, q1

    def back(q, d):
        return lax.rem(q + (n - d), n)

    def ahead(q, d):
        return lax.rem(q + d, n)

    def remote(src, dst, ssem, rsem, device):
        return pltpu.make_async_remote_copy(
            src_ref=src, dst_ref=dst, send_sem=ssem, recv_sem=rsem, device_id=device, device_id_type=MESH
        )

    w_copies = []
    for h in range(2):
        w_copies.append(pltpu.make_async_copy(win_hbm.at[pl.ds(h * half, half), :], win.at[h], w_sem.at[0, h]))
        w_copies.append(pltpu.make_async_copy(wout_hbm.at[:, pl.ds(h * half, half)], wout.at[h], w_sem.at[1, h]))
    w_copies = [w_copies[0], w_copies[2], w_copies[1], w_copies[3]]
    for copy in w_copies:
        copy.start()

    barrier = pltpu.get_barrier_semaphore()
    partners = [sibling, right, left]
    for d in range(1, n):
        for cc in range(2):
            partners.append(at(x + d, y, z, cc))
            partners.append(at(x, y + d, z, cc))
    for partner in partners:
        pl.semaphore_signal(barrier, inc=1, device_id=partner, device_id_type=MESH)
    pl.semaphore_wait(barrier, len(partners))

    pending = []

    def launch(copy):
        copy.start()
        pending.append(copy)
        return copy

    def drain(keep=0):
        while len(pending) > keep:
            pending.pop(0).wait_send()

    sources = (x_hbm, g_hbm)

    def s1(a):
        src = sources[a]
        for d in (2, 1, 3):
            if d >= n:
                continue
            launch(remote(src.at[:, pl.ds(0, half)], acts.at[a, 0, c, y, x], s1_ssem.at[a, 0, d], s1_rsem.at[a, c, d], at(x + d, y, z, 0)))
            launch(remote(src.at[:, pl.ds(half, half)], acts.at[a, 1, c, x, y], s1_ssem.at[a, 1, d], s1_rsem.at[a, c, d], at(x, y + d, z, 1)))
        theirs = src.at[:, pl.ds(pl.multiple_of(o * half, half), half)]
        mine = src.at[:, pl.ds(pl.multiple_of(c * half, half), half)]
        launch(remote(theirs, acts.at[a, o, c, r2, r1], s1_ssem.at[a, 0, 0], s1_rsem.at[a, c, 0], sibling))
        pltpu.make_async_copy(mine, acts.at[a, c, c, q2, q1], s1_rsem.at[a, c, 0]).start()

    def s2(a, t):
        for d in range(n):
            slot = acts.at[a, c, t, q2, back(q1, d)]
            pltpu.make_async_copy(slot, slot, s1_rsem.at[a, t, d]).wait()
        line = acts.at[a, c, t, q2]
        for d in (2, 1, 3):
            if d < n:
                launch(remote(line, line, s2_ssem.at[a, t, d], s2_rsem.at[a, t, d], line2(d)))
        launch(remote(line, line, sp_ssem.at[a, t, 0], sp_rsem.at[a, t, 0], sibling))

    def s3(a, t):
        for d in (1, 3, 2):
            if d >= n:
                continue
            line = acts.at[a, c, t, back(q2, d)]
            pltpu.make_async_copy(line, line, s2_rsem.at[a, t, d]).wait()
            launch(remote(line, line, sp_ssem.at[a, t, d], sp_rsem.at[a, t, d], sibling))
        for d in range(n):
            line = acts.at[a, o, t, back(r2, d)]
            pltpu.make_async_copy(line, line, sp_rsem.at[a, t, d]).wait()

    def rows_of(a, h, t):
        if h == 0:
            return acts[a, 0, t].reshape(n * n * 16, half)
        return jnp.concatenate([acts[a, 1, t, i, j] for j in range(n) for i in range(n)], axis=0)

    def partial(a, t):
        s = 2 * a + t
        rows = [rows_of(a, h, t) for h in range(2)]
        step = 256 if width % 256 == 0 else width
        for k in range(0, width, step):
            if a == 0:
                value = sum(contract(rows[h], win[h, :, k:k + step], 1, 0) for h in range(2))
            else:
                value = sum(contract(rows[h], wout[h, k:k + step, :], 1, 1) for h in range(2))
            part[s, :, :, k:k + step] = value.reshape(nz, -1, step)

    hz = nz // 2

    def rs_send(s, way, i, cols):
        ref = (s, way, i) if cols is None else (s, way, i, slice(None), cols)
        return remote(z_send.at[ref], z_recv.at[ref], z_ssem.at[s, way, i], z_rsem.at[s, way, i], (right, left)[way])

    rs = {}
    first_cols = (pl.ds(0, wmid), pl.ds(wmid, wmid))

    def rs_step(s, i):
        if i == 0:
            k = lax.rem(z + hz, nz)
            for way in range(2):
                cols = slice(way * wmid, (way + 1) * wmid)
                z_send[s, way, 0, :, cols] = part[s, k, :, cols].astype(BF)
                rs[s, way, 0] = launch(rs_send(s, way, 0, first_cols[way]))
            return
        if i < hz:
            for way in range(2):
                k = lax.rem(z + (hz - i if way == 0 else hz + i), nz)
                rs[s, way, i - 1].wait_recv()
                if i == 1:
                    for side in range(2):
                        cols = slice(side * wmid, (side + 1) * wmid)
                        value = part[s, k, :, cols]
                        if side == way:
                            value = value + z_recv[s, way, 0, :, cols].astype(F32)
                        z_send[s, way, i, :, cols] = value.astype(BF)
                else:
                    z_send[s, way, i] = (part[s, k] + z_recv[s, way, i - 1].astype(F32)).astype(BF)
                rs[s, way, i] = launch(rs_send(s, way, i, None))
            return
        rs[s, 0, hz - 1].wait_recv()
        rs[s, 1, hz - 1].wait_recv()
        total = part[s, z] + (z_recv[s, 0, hz - 1].astype(F32) + z_recv[s, 1, hz - 1].astype(F32))
        t = s % 2
        if s < 2:
            value, slope = gelu_parts(total)
            slope_ref[t] = slope
            wide[0, t, z] = value.astype(BF)
        else:
            wide[1, t, z] = (total * slope_ref[t]).astype(BF)

    ag = {}

    def ag_step(s, i):
        a, t = s // 2, s % 2
        if i > 0:
            ag[s, 0, i - 1].wait_recv()
            ag[s, 1, i - 1].wait_recv()
        if i == hz:
            return
        for way in range(2):
            k = lax.rem(z + (nz - i if way == 0 else i), nz)
            block = wide.at[a, t, k]
            if i == hz - 1:
                block = wide.at[a, t, k, pl.ds(16 * way, 16)]
            ag[s, way, i] = launch(remote(block, block, a_ssem.at[s, way, i], a_rsem.at[s, way, i], (right, left)[way]))

    sib = {}

    def product(s):
        a, t = s // 2, s % 2
        rows = wide[a, t].reshape(-1, width)
        for which, ref in ((o, oth_sum), (c, own_sum)):
            step = 256 if half % 256 == 0 else half
            for k in range(0, half, step):
                if a == 0:
                    value = contract(rows, wout[which, :, k:k + step], 1, 0)
                else:
                    value = contract(rows, win[which, k:k + step, :], 1, 1)
                ref[s, :, :, k:k + step] = value.reshape(n * n, 16, step)
            if ref is oth_sum:
                sib[s] = launch(remote(oth_sum.at[s], sib_sum.at[s], sib_ssem.at[s], sib_rsem.at[s], sibling))

    def block_of(i1, i2):
        return i1 * (1 + (n - 1) * c) + i2 * (n - (n - 1) * c)

    p1, p2 = {}, {}

    def phase1(s):
        sib[s].wait_recv()
        for d in (2, 1, 3):
            if d >= n:
                continue
            i1 = ahead(q1, d)
            for j in range(n):
                b = block_of(i1, j)
                p1_send[s, d - 1, j] = (own_sum[s, b] + sib_sum[s, b]).astype(BF)
            p1[s, d] = launch(remote(p1_send.at[s, d - 1], p1_recv.at[s, d - 1], p1_ssem.at[s, d], p1_rsem.at[s, d], line1(d)))

    def line_total(s, j):
        b = block_of(q1, j)
        value = own_sum[s, b] + sib_sum[s, b]
        for d in range(1, n):
            value = value + p1_recv[s, d - 1, j].astype(F32)
        return value

    def phase2(s):
        for d in range(1, n):
            p1[s, d].wait_recv()
        for d in (2, 1, 3):
            if d >= n:
                continue
            p2_send[s, d - 1] = line_total(s, ahead(q2, d))
            p2[s, d] = launch(remote(p2_send.at[s, d - 1], p2_recv.at[s, d - 1], p2_ssem.at[s, d], p2_rsem.at[s, d], line2(d)))

    results = (out_ref, gin_ref)

    def finish(s):
        a, t = s // 2, s % 2
        value = line_total(s, q2)
        for d in range(1, n):
            p2[s, d].wait_recv()
        for d in range(1, n):
            value = value + p2_recv[s, d - 1]
        value = value.astype(BF)

        @pl.when(c != t)
        def _():
            fin_send[a] = value
            remote(fin_send.at[a], fin_recv.at[a], fin_ssem.at[a], fin_rsem.at[a], sibling).start()

        @pl.when(c == t)
        def _():
            cols = slice(t * half, (t + 1) * half)
            results[a][:, cols] = value

    def collect(a):
        copy = remote(fin_send.at[a], fin_recv.at[a], fin_ssem.at[a], fin_rsem.at[a], sibling)
        copy.wait_send()
        copy.wait_recv()
        for t in range(2):
            @pl.when(c == t)
            def _():
                cols = slice((1 - t) * half, (2 - t) * half)
                results[a][:, cols] = fin_recv[a]

    gw_copies = []

    def grad_w_out(h):
        cols = jnp.concatenate([rows_of(1, h, t) for t in range(2)], axis=0)
        step = 256 if width % 256 == 0 else width
        for k in range(0, width, step):
            left_rows = wide[0, :, :, :, k:k + step].reshape(-1, step)
            gw_out[h, k:k + step, :] = (contract(left_rows, cols, 0, 0) * factor).astype(BF)
        copy = pltpu.make_async_copy(gw_out.at[h], gwout_hbm.at[:, pl.ds(h * half, half)], gw_sem.at[1, h])
        copy.start()
        gw_copies.append(copy)

    def grad_w_in(h):
        cols = wide[1].reshape(-1, width)
        step = 256 if half % 256 == 0 else half
        rows = jnp.concatenate([rows_of(0, h, t) for t in range(2)], axis=0)
        for k in range(0, half, step):
            gw_in[h, k:k + step, :] = (contract(rows[:, k:k + step], cols, 0, 0) * factor).astype(BF)
        copy = pltpu.make_async_copy(gw_in.at[h], gwin_hbm.at[pl.ds(h * half, half), :], gw_sem.at[0, h])
        copy.start()
        gw_copies.append(copy)

    s1(0)
    s2(0, 0)
    s2(0, 1)
    s1(1)
    s3(0, 0)
    w_copies[0].wait()
    w_copies[1].wait()
    partial(0, 0)
    rs_step(0, 0)
    s2(1, 0)
    s3(0, 1)
    partial(0, 1)
    rs_step(1, 0)
    s2(1, 1)
    rs_step(0, 1)
    s3(1, 0)
    w_copies[2].wait()
    w_copies[3].wait()
    partial(1, 0)
    rs_step(2, 0)
    rs_step(1, 1)
    rs_step(0, 2)
    s3(1, 1)
    partial(1, 1)
    rs_step(3, 0)
    rs_step(1, 2)
    rs_step(2, 1)
    rs_step(0, 3)
    rs_step(3, 1)
    rs_step(1, 3)
    rs_step(2, 2)
    rs_step(0, 4)
    ag_step(0, 0)
    rs_step(3, 2)
    rs_step(1, 4)
    ag_step(1, 0)
    rs_step(2, 3)
    ag_step(0, 1)
    rs_step(3, 3)
    ag_step(1, 1)
    rs_step(2, 4)
    ag_step(2, 0)
    ag_step(0, 2)
    rs_step(3, 4)
    ag_step(3, 0)
    ag_step(1, 2)
    ag_step(2, 1)
    ag_step(0, 3)
    ag_step(3, 1)
    ag_step(1, 3)
    ag_step(2, 2)
    ag_step(0, 4)
    product(0)
    ag_step(3, 2)
    ag_step(1, 4)
    product(1)
    ag_step(2, 3)
    phase1(0)
    ag_step(3, 3)
    phase1(1)
    ag_step(2, 4)
    product(2)
    phase2(0)
    ag_step(3, 4)
    product(3)
    phase1(2)
    phase2(1)
    phase1(3)
    grad_w_out(0)
    finish(0)
    phase2(2)
    grad_w_out(1)
    finish(1)
    phase2(3)
    grad_w_in(0)
    finish(2)
    grad_w_in(1)
    finish(3)
    drain()
    collect(0)
    collect(1)
    for copy in gw_copies:
        copy.wait()


def shards(n, nz, inputs, w_in, w_out, grad_out):
    rows, wide_cols = inputs.shape
    half = wide_cols // 2
    width = w_in.shape[1]
    tokens = 2 * n * n * rows
    chunk = n * n * rows // nz
    any_spec = pl.BlockSpec(memory_space=pl.ANY)
    vmem_spec = pl.BlockSpec(memory_space=pltpu.VMEM)
    dma = pltpu.SemaphoreType.DMA
    hz = nz // 2
    scratch = [
        pltpu.VMEM((2, 2, 2, n, n, rows, half), BF),
        pltpu.VMEM((2, half, width), BF),
        pltpu.VMEM((2, width, half), BF),
        pltpu.VMEM((4, nz, chunk, width), F32),
        pltpu.VMEM((4, 2, hz, chunk, width), BF),
        pltpu.VMEM((4, 2, hz, chunk, width), BF),
        pltpu.VMEM((2, chunk, width), F32),
        pltpu.VMEM((2, 2, nz, chunk, width), BF),
        pltpu.VMEM((4, n * n, rows, half), F32),
        pltpu.VMEM((4, n * n, rows, half), F32),
        pltpu.VMEM((4, n * n, rows, half), F32),
        pltpu.VMEM((4, n - 1, n, rows, half), BF),
        pltpu.VMEM((4, n - 1, n, rows, half), BF),
        pltpu.VMEM((4, n - 1, rows, half), F32),
        pltpu.VMEM((4, n - 1, rows, half), F32),
        pltpu.VMEM((2, rows, half), BF),
        pltpu.VMEM((2, rows, half), BF),
        pltpu.VMEM((2, half, width), BF),
        pltpu.VMEM((2, width, half), BF),
        dma((2, 2)), dma((2, 2)),
        dma((2, 2, n)), dma((2, 2, n)),
        dma((2, 2, n)), dma((2, 2, n)),
        dma((2, 2, n)), dma((2, 2, n)),
        dma((4, 2, hz)), dma((4, 2, hz)),
        dma((4, 2, hz)), dma((4, 2, hz)),
        dma((4,)), dma((4,)),
        dma((4, n)), dma((4, n)),
        dma((4, n)), dma((4, n)),
        dma((2,)), dma((2,)),
    ]
    return pl.pallas_call(
        functools.partial(body, n, nz, 1.0 / tokens ** 0.5),
        name="ffn",
        out_shape=(
            jax.ShapeDtypeStruct(inputs.shape, BF),
            jax.ShapeDtypeStruct(inputs.shape, BF),
            jax.ShapeDtypeStruct(w_in.shape, BF),
            jax.ShapeDtypeStruct(w_out.shape, BF),
        ),
        in_specs=[any_spec] * 4,
        out_specs=(vmem_spec, vmem_spec, any_spec, any_spec),
        scratch_shapes=scratch,
        compiler_params=pltpu.CompilerParams(
            collective_id=0, has_side_effects=True, vmem_limit_bytes=60 * 2 ** 20
        ),
        cost_estimate=pl.CostEstimate(
            flops=12 * tokens * wide_cols * width, bytes_accessed=8 * wide_cols * width, transcendentals=0
        ),
    )(inputs, w_in, w_out, grad_out)


def solution(mesh):
    n, nz = mesh.shape["row"], mesh.shape["col"]
    in_specs = (
        P(("row", "depth"), "col"),
        P("col", ("row", "depth")),
        P(("row", "depth"), "col"),
        P(("row", "depth"), "col"),
    )
    out_specs = (
        P(("row", "depth"), "col"),
        P(("row", "depth"), "col"),
        P("col", ("row", "depth")),
        P(("row", "depth"), "col"),
    )
    return jax.shard_map(
        functools.partial(shards, n, nz), mesh=mesh, in_specs=in_specs, out_specs=out_specs, check_vma=False
    )
```

```python
import functools

import jax
import jax.numpy as jnp
from jax import lax
from jax.experimental import pallas as pl
from jax.experimental.pallas import tpu as pltpu
from jax.sharding import PartitionSpec as P

MESH = pl.DeviceIdType.MESH
BF = jnp.bfloat16
F32 = jnp.float32


SHORT_SUMS = (0,)
SHORT_GATHERS = ()

SCHEDULE = (
    ("s1", 0), ("s1", 1), ("s2", 0, 1), ("s2", 0, 0), ("s2", 1, 0), ("s2", 1, 1), ("s3", 0, 1), ("s4", 0, 1),
    ("weights", 0), ("partial", 0, 1), ("s3", 0, 0), ("rs_step", 1, 0), ("s4", 0, 0), ("partial", 0, 0),
    ("rs_step", 0, 0), ("s3", 1, 0), ("rs_step", 1, 1), ("s3", 1, 1), ("s4", 1, 0), ("weights", 1), ("partial", 1, 0),
    ("rs_step", 2, 0), ("s4", 1, 1), ("partial", 1, 1), ("rs_step", 3, 0), ("rs_step", 0, 1), ("rs_step", 1, 2),
    ("rs_step", 2, 1), ("rs_step", 3, 1), ("rs_step", 0, 2), ("ag_step", 0, 0), ("rs_step", 1, 3), ("rs_step", 2, 2),
    ("rs_step", 3, 2), ("ag_step", 0, 1), ("rs_step", 1, 4), ("ag_step", 1, 0), ("rs_step", 2, 3), ("rs_step", 3, 3),
    ("ag_step", 0, 2), ("ag_step", 1, 1), ("rs_step", 2, 4), ("ag_step", 2, 0), ("rs_step", 3, 4), ("ag_step", 3, 0),
    ("ag_step", 0, 3), ("product", 0, True), ("ag_step", 1, 2), ("ag_step", 2, 1), ("ag_step", 3, 1),
    ("ag_step", 0, 4), ("product", 0, False), ("ag_step", 1, 3), ("product", 1, True), ("spread", 0),
    ("ag_step", 3, 2), ("ag_step", 2, 2), ("ag_step", 1, 4), ("grad_w_out", 1), ("product", 1, False),
    ("grad_w_out", 0), ("ag_step", 3, 3), ("product", 3, True), ("spread", 1), ("ag_step", 2, 3),
    ("product", 2, True), ("finish", 0), ("ag_step", 3, 4), ("product", 3, False), ("ag_step", 2, 4),
    ("product", 2, False), ("spread", 3), ("grad_w_in", 1), ("spread", 2), ("finish", 1), ("grad_w_in", 0),
    ("collect", 0), ("finish", 3), ("finish", 2), ("collect", 1), ("drain",),
)


def gelu_parts(hidden):
    inner = 0.7978845608 * (hidden + 0.044715 * hidden * hidden * hidden)
    tangent = jnp.tanh(inner)
    value = 0.5 * hidden * (1.0 + tangent)
    slope = 0.5 * (1.0 + tangent) + 0.5 * hidden * (1.0 - tangent * tangent) * 0.7978845608 * (
        1.0 + 3.0 * 0.044715 * hidden * hidden
    )
    return (value, slope)


def contract(left, right, left_dim, right_dim):
    return lax.dot_general(
        left, right, (((left_dim,), (right_dim,)), ((), ())), preferred_element_type=F32
    )


def body(
    n, nz, factor,
    x_hbm, win_hbm, wout_hbm, g_hbm,
    out_ref, gin_ref, gw_in, gw_out,
    acts, win, wout, part, z_send, z_recv, slope_ref, wide,
    own_sum, oth_sum, sib_sum, out_send, out_recv, fin_send, fin_recv,
    own_rows,
    w_sem, x_sem, s1_rsem, s2_rsem, sp_rsem, z_rsem, a_rsem, sib_rsem, out_rsem, fin_rsem, send_sem,
):
    y = lax.axis_index("row")
    z = lax.axis_index("col")
    depth = lax.axis_index("depth")
    x, c = depth // 2, lax.rem(depth, 2)
    o = 1 - c
    half = win.shape[1]
    quarter = half // 2
    width = win.shape[2]
    wmid = width // 2

    def at(xx, yy, zz, cc):
        return (lax.rem(yy, n), lax.rem(zz, nz), lax.rem(xx, n) * 2 + cc)

    sibling = at(x, y, z, o)
    hop = [[at(x, y, z + d, c) for d in (1, nz - 1)], [at(x, y, z + d, c) for d in (2, nz - 2)]]

    places = ((x, y), (y, x))

    def line(q, axis, d):
        return at(x + d, y, z, c) if q == axis else at(x, y + d, z, c)

    def back(q, d):
        return lax.rem(q + (n - d), n)

    def ahead(q, d):
        return lax.rem(q + d, n)

    def remote(src, dst, ssem, rsem, device):
        return pltpu.make_async_remote_copy(
            src_ref=src, dst_ref=dst, send_sem=ssem, recv_sem=rsem, device_id=device, device_id_type=MESH
        )

    x_copies, w_copies = [], []
    for a, src in enumerate((x_hbm, g_hbm)):
        for h in range(2):
            for q in range(2):
                cols = pl.ds(h * half + q * quarter, quarter)
                x_copies.append(pltpu.make_async_copy(src.at[:, cols], own_rows.at[a, h, q], x_sem.at[a]))
    for h in range(2):
        w_copies.append(pltpu.make_async_copy(win_hbm.at[pl.ds(h * half, half), :], win.at[h], w_sem.at[0]))
        w_copies.append(pltpu.make_async_copy(wout_hbm.at[:, pl.ds(h * half, half)], wout.at[h], w_sem.at[1]))
    for copy in x_copies + w_copies:
        copy.start()

    barrier = pltpu.get_barrier_semaphore()
    partners = [sibling]
    for d in sorted({1, 2, nz - 2, nz - 1}):
        partners.append(at(x, y, z + d, c))
    for d in range(1, n):
        for cc in range(2):
            partners.append(at(x + d, y, z, cc))
            partners.append(at(x, y + d, z, cc))
        for e in range(1, n):
            partners.append(at(x + d, y + e, z, c))
    for partner in partners:
        pl.semaphore_signal(barrier, inc=1, device_id=partner, device_id_type=MESH)
    pl.semaphore_wait(barrier, len(partners))

    def launch(copy):
        copy.start()
        return copy

    def arrived(ref, sem):
        pltpu.make_async_copy(ref, ref, sem).wait()

    def drain():
        blocks = own_sum
        for k, ref in enumerate((
            blocks.at[0, pl.ds(0, 2 * n - 1)],
            blocks.at[pl.ds(0, 2), pl.ds(0, n * (n - 1))],
            blocks.at[pl.ds(0, 2)],
            part.at[pl.ds(0, 2), pl.ds(0, nz - 1)],
            part.at[pl.ds(0, 2), pl.ds(0, nz - 1)],
            blocks.at[pl.ds(0, 2), pl.ds(0, n * n - 1)],
            fin_send,
            blocks.at[0], blocks.at[1], blocks.at[2], blocks.at[3],
        )):
            arrived(ref, send_sem.at[k])

    def s1(a):
        arrived(own_rows.at[a], x_sem.at[a])
        for d in (2, 1, 3):
            if d >= n:
                continue
            for h in range(2):
                for q in range(2):
                    first, second = places[q]
                    there = at(x + d, y, z, h) if q == 0 else at(x, y + d, z, h)
                    launch(remote(
                        own_rows.at[a, h, q], acts.at[a, h, q, c, second, first], send_sem.at[0], s1_rsem.at[a, c, q], there
                    ))
        for q in range(2):
            first, second = places[q]
            launch(remote(
                own_rows.at[a, o, q], acts.at[a, o, q, c, second, first], send_sem.at[0], s1_rsem.at[a, c, q], sibling
            ))
            launch(pltpu.make_async_copy(
                own_rows.at[a, c, q], acts.at[a, c, q, c, second, first], s1_rsem.at[a, c, q]
            ))

    def s2(a, t):
        for q in range(2):
            row = acts.at[a, c, q, t, places[q][1]]
            arrived(row, s1_rsem.at[a, t, q])
            for d in (2, 1, 3):
                if d < n:
                    launch(remote(row, row, send_sem.at[1], s2_rsem.at[a, t, q, d - 1], line(q, 1, d)))
            launch(remote(row, row, send_sem.at[2], sp_rsem.at[a, t], sibling))

    def s3(a, t):
        for d in (1, 3, 2):
            if d >= n:
                continue
            for q in range(2):
                row = acts.at[a, c, q, t, back(places[q][1], d)]
                arrived(row, s2_rsem.at[a, t, q, d - 1])
                launch(remote(row, row, send_sem.at[2], sp_rsem.at[a, t], sibling))

    def s4(a, t):
        arrived(acts.at[a, o, :, t], sp_rsem.at[a, t])

    def rows_of(a, h, t):
        across = [acts[a, h, 0, t].reshape(n * n * 16, quarter)]
        across.append(jnp.concatenate([acts[a, h, 1, t, i, j] for j in range(n) for i in range(n)], axis=0))
        return jnp.concatenate(across, axis=1)

    def partial(a, t):
        s = 2 * a + t
        rows = [rows_of(a, h, t) for h in range(2)]
        step = 256 if width % 256 == 0 else width
        for k in range(0, width, step):
            if a == 0:
                value = sum(contract(rows[h], win[h, :, k:k + step], 1, 0) for h in range(2))
            else:
                value = sum(contract(rows[h], wout[h, k:k + step, :], 1, 1) for h in range(2))
            part[s, :, :, k:k + step] = value.reshape(nz, -1, step)

    hz = nz // 2
    signs = (1, -1)

    def chunk_at(d):
        return lax.rem(z + (d + nz), nz)

    def rs_send(s, i, way, far):
        cols = (slice(None), pl.ds(0, wmid)) if i == 0 else ()
        ref = (s, way, i) + cols
        launch(remote(z_send.at[ref], z_recv.at[ref], send_sem.at[3], z_rsem.at[s, i], hop[far][way]))

    def rs_wait(s, i):
        ref = z_recv.at[s, :, 0, :, pl.ds(0, wmid)] if i == 0 else z_recv.at[s, :, i]
        arrived(ref, z_rsem.at[s, i])

    def rs_first(s, far):
        for way in range(2):
            z_send[s, way, 0, :, :wmid] = part[s, chunk_at(hz), :, way * wmid:(way + 1) * wmid].astype(BF)
            rs_send(s, 0, way, far)

    def with_half(s, way, value):
        half_in = z_recv[s, way, 0, :, :wmid].astype(F32)
        if way == 0:
            return jnp.concatenate([value[:, :wmid] + half_in, value[:, wmid:]], axis=1)
        return jnp.concatenate([value[:, :wmid], value[:, wmid:] + half_in], axis=1)

    def settle(s, total):
        t = s % 2
        if s < 2:
            value, slope = gelu_parts(total)
            slope_ref[t] = slope
            wide[0, t, z] = value.astype(BF)
        else:
            wide[1, t, z] = (total * slope_ref[t]).astype(BF)

    def rs_chain(s, i):
        if i == 0:
            rs_first(s, 0)
        elif i < hz:
            rs_wait(s, i - 1)
            for way in range(2):
                value = part[s, chunk_at(signs[way] * (hz - i))]
                if i == 1:
                    value = with_half(s, way, value)
                else:
                    value = value + z_recv[s, way, i - 1].astype(F32)
                z_send[s, way, i] = value.astype(BF)
                rs_send(s, i, way, 0)
        else:
            rs_wait(s, hz - 1)
            settle(s, part[s, z] + (z_recv[s, 0, hz - 1].astype(F32) + z_recv[s, 1, hz - 1].astype(F32)))

    def rs_short(s, i):
        if i == 0:
            for way in range(2):
                z_send[s, way, 1] = part[s, chunk_at(signs[way] * 3)].astype(BF)
                rs_send(s, 1, way, 0)
            rs_first(s, 1)
            for way in range(2):
                z_send[s, way, 2] = part[s, chunk_at(signs[way])].astype(BF)
                rs_send(s, 2, way, 0)
        elif i == 1:
            rs_wait(s, 1)
            rs_wait(s, 0)
            for way in range(2):
                value = part[s, chunk_at(signs[way] * 2)] + z_recv[s, way, 1].astype(F32)
                z_send[s, way, 3] = with_half(s, way, value).astype(BF)
                rs_send(s, 3, way, 1)
        else:
            rs_wait(s, 2)
            rs_wait(s, 3)
            total = part[s, z]
            for k in (2, 3):
                total = total + (z_recv[s, 0, k].astype(F32) + z_recv[s, 1, k].astype(F32))
            settle(s, total)

    def ag_block(s, way, i):
        block = (s // 2, s % 2, chunk_at(-signs[way] * i))
        return block + (pl.ds(16 * way, 16),) if i == hz else block

    def ag_send(s, way, i, far):
        block = wide.at[ag_block(s, way, i - 1 - far) + ((pl.ds(16 * way, 16),) if i == hz else ())]
        launch(remote(block, block, send_sem.at[4], a_rsem.at[s, way, i - 1], hop[far][way]))

    def ag_wait(s, i):
        for way in range(2):
            arrived(wide.at[ag_block(s, way, i)], a_rsem.at[s, way, i - 1])

    def ag_chain(s, i):
        if i > 0:
            ag_wait(s, i)
        if i < hz:
            for way in range(2):
                ag_send(s, way, i + 1, 0)

    def ag_short(s, i):
        if i == 0:
            for way in range(2):
                ag_send(s, way, 2, 1)
            for way in range(2):
                ag_send(s, way, 1, 0)
        elif i == 1:
            ag_wait(s, 2)
            for way in range(2):
                ag_send(s, way, 3, 0)
            for way in range(2):
                ag_send(s, way, 4, 1)
        else:
            for k in (1, 3, 4):
                ag_wait(s, k)

    def rs_step(s, i):
        (rs_short if s in SHORT_SUMS else rs_chain)(s, i)

    def ag_step(s, i):
        (ag_short if s in SHORT_GATHERS else ag_chain)(s, i)

    def product(s, early):
        a, t = s // 2, s % 2
        near = hz - 2
        if early is None:
            chunks = list(range(nz))
        else:
            chunks = [chunk_at(d) for d in (range(-near, near + 1) if early else range(near + 1, nz - near))]
        rows = jnp.concatenate([wide[a, t, k] for k in chunks], axis=0)
        each = rows.shape[0] // len(chunks)
        per = each // 16
        for which, ref in ((o, oth_sum), (c, own_sum)):
            step = 256 if half % 256 == 0 else half
            for k in range(0, half, step):
                if a == 0:
                    value = contract(rows, wout[which, :, k:k + step], 1, 0)
                else:
                    value = contract(rows, win[which, k:k + step, :], 1, 1)
                for i, chunk in enumerate(chunks):
                    ref[s, pl.ds(chunk * per, per), :, k:k + step] = value[i * each:(i + 1) * each].reshape(per, 16, step)
            if ref is oth_sum:
                for chunk in chunks:
                    there = pl.ds(chunk * per, per)
                    launch(remote(
                        oth_sum.at[s, there], sib_sum.at[s, there], send_sem.at[7 + s], sib_rsem.at[s], sibling
                    ))

    def spread(s):
        arrived(sib_sum.at[s], sib_rsem.at[s])
        for e in (2, 1, 3, 0):
            for d in (2, 1, 3, 0):
                if (d, e) == (0, 0) or d >= n or e >= n:
                    continue
                b = ahead(y, e) * n + ahead(x, d)
                k = e * n + d - 1
                out_send[s, k] = (own_sum[s, b] + sib_sum[s, b]).astype(BF)
                launch(remote(out_send.at[s, k], out_recv.at[s, k], send_sem.at[5], out_rsem.at[s], at(x + d, y + e, z, c)))

    results = (out_ref, gin_ref)

    def finish(s):
        a, t = s // 2, s % 2
        value = own_sum[s, y * n + x] + sib_sum[s, y * n + x]
        arrived(out_recv.at[s], out_rsem.at[s])
        for k in range(n * n - 1):
            value = value + out_recv[s, k].astype(F32)
        value = value.astype(BF)

        @pl.when(c != t)
        def _():
            fin_send[a] = value
            remote(fin_send.at[a], fin_recv.at[a], send_sem.at[6], fin_rsem.at[a], sibling).start()

        @pl.when(c == t)
        def _():
            cols = slice(t * half, (t + 1) * half)
            results[a][:, cols] = value

    def collect(a):
        arrived(fin_recv.at[a], fin_rsem.at[a])
        for t in range(2):
            @pl.when(c == t)
            def _():
                cols = slice((1 - t) * half, (2 - t) * half)
                results[a][:, cols] = fin_recv[a]

    def grad_w_out(h):
        cols = jnp.concatenate([rows_of(1, h, t) for t in range(2)], axis=0)
        step = 256 if width % 256 == 0 else width
        for k in range(0, width, step):
            left_rows = wide[0, :, :, :, k:k + step].reshape(-1, step)
            gw_out[h, k:k + step, :] = (contract(left_rows, cols, 0, 0) * factor).astype(BF)

    def grad_w_in(h):
        cols = wide[1].reshape(-1, width)
        step = 256 if half % 256 == 0 else half
        rows = jnp.concatenate([rows_of(0, h, t) for t in range(2)], axis=0)
        for k in range(0, half, step):
            gw_in[h, k:k + step, :] = (contract(rows[:, k:k + step], cols, 0, 0) * factor).astype(BF)

    def weights(a):
        arrived((win, wout)[a], w_sem.at[a])

    steps = {
        "s1": s1, "s2": s2, "s3": s3, "s4": s4, "weights": weights, "partial": partial, "rs_step": rs_step, "ag_step": ag_step,
        "product": product, "spread": spread, "finish": finish, "collect": collect, "drain": drain,
        "grad_w_out": grad_w_out, "grad_w_in": grad_w_in,
    }
    for step, *place in SCHEDULE:
        steps[step](*place)


def hand_over(out, gin, gw_in, gw_out, out_to, gin_to, gw_in_to, gw_out_to, sem):
    half = gw_in.shape[1]
    parts = 4
    step = half // parts
    copies = []
    for h in range(2):
        for p in range(parts):
            k = len(copies)
            copies.append(pltpu.make_async_copy(
                gw_in.at[h, pl.ds(p * step, step)], gw_in_to.at[pl.ds(h * half + p * step, step), :], sem.at[k]
            ))
            copies.append(pltpu.make_async_copy(
                gw_out.at[h, pl.ds(p * step, step)], gw_out_to.at[pl.ds(p * step, step), pl.ds(h * half, half)], sem.at[k + 1]
            ))
    copies.append(pltpu.make_async_copy(out, out_to, sem.at[len(copies)]))
    copies.append(pltpu.make_async_copy(gin, gin_to, sem.at[len(copies)]))
    for copy in copies:
        copy.start()
    for copy in copies:
        copy.wait()


def shards(n, nz, inputs, w_in, w_out, grad_out):
    rows, wide_cols = inputs.shape
    half = wide_cols // 2
    quarter = half // 2
    width = w_in.shape[1]
    tokens = 2 * n * n * rows
    chunk = n * n * rows // nz
    any_spec = pl.BlockSpec(memory_space=pl.ANY)
    vmem_spec = pl.BlockSpec(memory_space=pltpu.VMEM)
    dma = pltpu.SemaphoreType.DMA
    hz = nz // 2
    scratch = [
        pltpu.VMEM((2, 2, 2, 2, n, n, rows, quarter), BF),
        pltpu.VMEM((2, half, width), BF),
        pltpu.VMEM((2, width, half), BF),
        pltpu.VMEM((4, nz, chunk, width), F32),
        pltpu.VMEM((4, 2, hz, chunk, width), BF),
        pltpu.VMEM((4, 2, hz, chunk, width), BF),
        pltpu.VMEM((2, chunk, width), F32),
        pltpu.VMEM((2, 2, nz, chunk, width), BF),
        pltpu.VMEM((4, n * n, rows, half), F32),
        pltpu.VMEM((4, n * n, rows, half), F32),
        pltpu.VMEM((4, n * n, rows, half), F32),
        pltpu.VMEM((4, n * n - 1, rows, half), BF),
        pltpu.VMEM((4, n * n - 1, rows, half), BF),
        pltpu.VMEM((2, rows, half), BF),
        pltpu.VMEM((2, rows, half), BF),
        pltpu.VMEM((2, 2, 2, rows, quarter), BF),
        dma((2,)), dma((2,)), dma((2, 2, 2)), dma((2, 2, 2, n - 1)), dma((2, 2)), dma((4, hz)), dma((4, 2, hz)),
        dma((4,)), dma((4,)), dma((2,)), dma((11,)),
    ]
    results = pl.pallas_call(
        functools.partial(body, n, nz, 1.0 / tokens ** 0.5),
        name="ffn",
        out_shape=(
            pltpu.VMEM(inputs.shape, BF),
            pltpu.VMEM(inputs.shape, BF),
            pltpu.VMEM((2, half, width), BF),
            pltpu.VMEM((2, width, half), BF),
        ),
        in_specs=[any_spec] * 4,
        out_specs=(vmem_spec,) * 4,
        scratch_shapes=scratch,
        compiler_params=pltpu.CompilerParams(
            collective_id=0, has_side_effects=True, vmem_limit_bytes=48 * 2 ** 20
        ),
        cost_estimate=pl.CostEstimate(
            flops=12 * tokens * wide_cols * width, bytes_accessed=8 * wide_cols * width, transcendentals=0
        ),
    )(*(pltpu.with_memory_space_constraint(r, pltpu.HBM) for r in (inputs, w_in, w_out, grad_out)))
    return pl.pallas_call(
        hand_over,
        name="hand_over",
        out_shape=tuple(jax.ShapeDtypeStruct(a.shape, BF) for a in (inputs, inputs, w_in, w_out)),
        in_specs=[vmem_spec] * 4,
        out_specs=[any_spec] * 4,
        scratch_shapes=[dma((18,))],
        compiler_params=pltpu.CompilerParams(vmem_limit_bytes=4 * 2 ** 20),
    )(*(pltpu.with_memory_space_constraint(r, pltpu.VMEM) for r in results))


def solution(mesh):
    n, nz = mesh.shape["row"], mesh.shape["col"]
    in_specs = (
        P(("row", "depth"), "col"),
        P("col", ("row", "depth")),
        P(("row", "depth"), "col"),
        P(("row", "depth"), "col"),
    )
    out_specs = (
        P(("row", "depth"), "col"),
        P(("row", "depth"), "col"),
        P("col", ("row", "depth")),
        P(("row", "depth"), "col"),
    )
    return jax.shard_map(
        functools.partial(shards, n, nz), mesh=mesh, in_specs=in_specs, out_specs=out_specs, check_vma=False
    )
```

```python
import functools

import jax
import jax.numpy as jnp
from jax import lax
from jax.experimental import pallas as pl
from jax.experimental.pallas import tpu as pltpu
from jax.sharding import PartitionSpec as P

MESH = pl.DeviceIdType.MESH
BF = jnp.bfloat16
F32 = jnp.float32


SHORT_SUMS = (0,)
SHORT_GATHERS = ()

SCHEDULE = (
    ("s1", 0), ("s1", 1), ("s2", 0, 1), ("s2", 0, 0), ("s2", 1, 1), ("s2", 1, 0), ("s3", 0, 1), ("weights", 0),
    ("partial", 0, 1, False), ("s4", 0, 1), ("partial", 0, 1, True), ("s3", 0, 0), ("partial", 0, 0, False),
    ("rs_step", 1, 0), ("s4", 0, 0), ("partial", 0, 0, True), ("rs_step", 0, 0), ("s3", 1, 1), ("weights", 1),
    ("partial", 1, 1, False), ("s4", 1, 1), ("rs_step", 1, 1), ("s3", 1, 0), ("partial", 1, 0, False),
    ("partial", 1, 1, True), ("s4", 1, 0), ("partial", 1, 0, True), ("rs_step", 2, 0), ("rs_step", 3, 0),
    ("rs_step", 0, 1), ("rs_step", 1, 2), ("rs_step", 2, 1), ("rs_step", 3, 1), ("rs_step", 0, 2), ("ag_step", 0, 0),
    ("rs_step", 1, 3), ("rs_step", 2, 2), ("rs_step", 3, 2), ("ag_step", 0, 1), ("rs_step", 1, 4), ("ag_step", 1, 0),
    ("rs_step", 2, 3), ("rs_step", 3, 3), ("ag_step", 0, 2), ("ag_step", 1, 1), ("rs_step", 2, 4), ("ag_step", 2, 0),
    ("rs_step", 3, 4), ("ag_step", 3, 0), ("ag_step", 0, 3), ("product", 0, True), ("ag_step", 1, 2),
    ("ag_step", 2, 1), ("spread", 0, True), ("ag_step", 3, 1), ("ag_step", 0, 4), ("product", 0, False),
    ("ag_step", 1, 3), ("product", 1, True), ("ag_step", 2, 2), ("spread", 0, False), ("ag_step", 3, 2),
    ("spread", 1, True), ("ag_step", 1, 4), ("product", 1, False), ("grad_w_out", 0), ("ag_step", 2, 3),
    ("product", 2, True), ("spread", 1, False), ("ag_step", 3, 3), ("finish", 0), ("product", 3, True),
    ("spread", 2, True), ("ag_step", 2, 4), ("product", 2, False), ("spread", 3, True), ("ag_step", 3, 4),
    ("grad_w_in", 0), ("product", 3, False), ("spread", 2, False), ("finish", 1), ("grad_w_in", 1), ("collect", 0),
    ("grad_w_out", 1), ("spread", 3, False), ("finish", 2), ("finish", 3), ("collect", 1), ("drain",),
)


def gelu_parts(hidden):
    inner = 0.7978845608 * (hidden + 0.044715 * hidden * hidden * hidden)
    tangent = jnp.tanh(inner)
    value = 0.5 * hidden * (1.0 + tangent)
    slope = 0.5 * (1.0 + tangent) + 0.5 * hidden * (1.0 - tangent * tangent) * 0.7978845608 * (
        1.0 + 3.0 * 0.044715 * hidden * hidden
    )
    return (value, slope)


def contract(left, right, left_dim, right_dim):
    return lax.dot_general(
        left, right, (((left_dim,), (right_dim,)), ((), ())), preferred_element_type=F32
    )


def body(
    n, nz, factor,
    x_hbm, win_hbm, wout_hbm, g_hbm,
    out_ref, gin_ref, gw_in, gw_out,
    acts, win, wout, part, z_send, z_recv, slope_ref, wide,
    own_sum, oth_sum, sib_sum, out_send, out_recv, fin_send, fin_recv,
    own_rows,
    w_sem, x_sem, s1_rsem, s2_rsem, sp_rsem, z_rsem, a_rsem, sib_rsem, out_rsem, fin_rsem, send_sem,
):
    y = lax.axis_index("row")
    z = lax.axis_index("col")
    depth = lax.axis_index("depth")
    x, c = depth // 2, lax.rem(depth, 2)
    o = 1 - c
    half = win.shape[1]
    quarter = half // 2
    width = win.shape[2]
    wmid = width // 2

    def at(xx, yy, zz, cc):
        return (lax.rem(yy, n), lax.rem(zz, nz), lax.rem(xx, n) * 2 + cc)

    sibling = at(x, y, z, o)
    hop = [[at(x, y, z + d, c) for d in (1, nz - 1)], [at(x, y, z + d, c) for d in (2, nz - 2)]]

    places = ((x, y), (y, x))

    def line(q, axis, d):
        return at(x + d, y, z, c) if q == axis else at(x, y + d, z, c)

    def back(q, d):
        return lax.rem(q + (n - d), n)

    def ahead(q, d):
        return lax.rem(q + d, n)

    def remote(src, dst, ssem, rsem, device):
        return pltpu.make_async_remote_copy(
            src_ref=src, dst_ref=dst, send_sem=ssem, recv_sem=rsem, device_id=device, device_id_type=MESH
        )

    x_copies, w_copies = [], []
    for a, src in enumerate((x_hbm, g_hbm)):
        for h in range(2):
            for q in range(2):
                cols = pl.ds(h * half + q * quarter, quarter)
                x_copies.append(pltpu.make_async_copy(src.at[:, cols], own_rows.at[a, h, q], x_sem.at[a]))
    for h in range(2):
        w_copies.append(pltpu.make_async_copy(win_hbm.at[pl.ds(h * half, half), :], win.at[h], w_sem.at[0]))
        w_copies.append(pltpu.make_async_copy(wout_hbm.at[:, pl.ds(h * half, half)], wout.at[h], w_sem.at[1]))
    for copy in x_copies:
        copy.start()

    barrier = pltpu.get_barrier_semaphore()
    partners = [sibling]
    for d in sorted({1, 2, nz - 2, nz - 1}):
        partners.append(at(x, y, z + d, c))
    for d in range(1, n):
        for cc in range(2):
            partners.append(at(x + d, y, z, cc))
            partners.append(at(x, y + d, z, cc))
        for e in range(1, n):
            partners.append(at(x + d, y + e, z, c))
    for partner in partners:
        pl.semaphore_signal(barrier, inc=1, device_id=partner, device_id_type=MESH)
    pl.semaphore_wait(barrier, len(partners))

    def launch(copy):
        copy.start()
        return copy

    def arrived(ref, sem):
        pltpu.make_async_copy(ref, ref, sem).wait()

    def drain():
        blocks = own_sum
        for k, ref in enumerate((
            blocks.at[0, pl.ds(0, 2 * n - 1)],
            blocks.at[pl.ds(0, 2), pl.ds(0, n * (n - 1))],
            blocks.at[pl.ds(0, 2)],
            part.at[pl.ds(0, 2), pl.ds(0, nz - 1)],
            part.at[pl.ds(0, 2), pl.ds(0, nz - 1)],
            blocks.at[pl.ds(0, 2), pl.ds(0, n * n - 1)],
            fin_send,
            blocks.at[0], blocks.at[1], blocks.at[2], blocks.at[3],
        )):
            arrived(ref, send_sem.at[k])

    def s1(a):
        arrived(own_rows.at[a], x_sem.at[a])
        for d in (2, 1, 3):
            if d >= n:
                continue
            for h in range(2):
                for q in range(2):
                    first, second = places[q]
                    there = at(x + d, y, z, h) if q == 0 else at(x, y + d, z, h)
                    launch(remote(
                        own_rows.at[a, h, q], acts.at[a, h, q, c, second, first], send_sem.at[0], s1_rsem.at[a, c, q], there
                    ))
        for q in range(2):
            first, second = places[q]
            launch(remote(
                own_rows.at[a, o, q], acts.at[a, o, q, c, second, first], send_sem.at[0], s1_rsem.at[a, c, q], sibling
            ))
            launch(pltpu.make_async_copy(
                own_rows.at[a, c, q], acts.at[a, c, q, c, second, first], s1_rsem.at[a, c, q]
            ))
        if a == 0:
            for copy in w_copies:
                copy.start()

    def s2(a, t):
        for q in range(2):
            row = acts.at[a, c, q, t, places[q][1]]
            arrived(row, s1_rsem.at[a, t, q])
            for d in (2, 1, 3):
                if d < n:
                    launch(remote(row, row, send_sem.at[1], s2_rsem.at[a, t, q, d - 1], line(q, 1, d)))
            launch(remote(row, row, send_sem.at[2], sp_rsem.at[a, t], sibling))

    def s3(a, t):
        for d in (1, 3, 2):
            if d >= n:
                continue
            for q in range(2):
                row = acts.at[a, c, q, t, back(places[q][1], d)]
                arrived(row, s2_rsem.at[a, t, q, d - 1])
                launch(remote(row, row, send_sem.at[2], sp_rsem.at[a, t], sibling))

    def s4(a, t):
        arrived(acts.at[a, o, :, t], sp_rsem.at[a, t])

    def rows_of(a, h, t):
        across = [acts[a, h, 0, t].reshape(n * n * 16, quarter)]
        across.append(jnp.concatenate([acts[a, h, 1, t, i, j] for j in range(n) for i in range(n)], axis=0))
        return jnp.concatenate(across, axis=1)

    def partial(a, t, theirs):
        s = 2 * a + t
        h = o if theirs else c
        rows = rows_of(a, h, t)
        step = 256 if width % 256 == 0 else width
        for k in range(0, width, step):
            if a == 0:
                value = contract(rows, win[h, :, k:k + step], 1, 0)
            else:
                value = contract(rows, wout[h, k:k + step, :], 1, 1)
            value = value.reshape(nz, -1, step)
            if theirs:
                value = value + part[s, :, :, k:k + step]
            part[s, :, :, k:k + step] = value

    hz = nz // 2
    signs = (1, -1)

    def chunk_at(d):
        return lax.rem(z + (d + nz), nz)

    def rs_send(s, i, way, far):
        cols = (slice(None), pl.ds(0, wmid)) if i == 0 else ()
        ref = (s, way, i) + cols
        launch(remote(z_send.at[ref], z_recv.at[ref], send_sem.at[3], z_rsem.at[s, i], hop[far][way]))

    def rs_wait(s, i):
        ref = z_recv.at[s, :, 0, :, pl.ds(0, wmid)] if i == 0 else z_recv.at[s, :, i]
        arrived(ref, z_rsem.at[s, i])

    def rs_first(s, far):
        for way in range(2):
            z_send[s, way, 0, :, :wmid] = part[s, chunk_at(hz), :, way * wmid:(way + 1) * wmid].astype(BF)
            rs_send(s, 0, way, far)

    def with_half(s, way, value):
        half_in = z_recv[s, way, 0, :, :wmid].astype(F32)
        if way == 0:
            return jnp.concatenate([value[:, :wmid] + half_in, value[:, wmid:]], axis=1)
        return jnp.concatenate([value[:, :wmid], value[:, wmid:] + half_in], axis=1)

    def settle(s, total):
        t = s % 2
        if s < 2:
            value, slope = gelu_parts(total)
            slope_ref[t] = slope
            wide[0, t, z] = value.astype(BF)
        else:
            wide[1, t, z] = (total * slope_ref[t]).astype(BF)

    def rs_chain(s, i):
        if i == 0:
            rs_first(s, 0)
        elif i < hz:
            rs_wait(s, i - 1)
            for way in range(2):
                value = part[s, chunk_at(signs[way] * (hz - i))]
                if i == 1:
                    value = with_half(s, way, value)
                else:
                    value = value + z_recv[s, way, i - 1].astype(F32)
                z_send[s, way, i] = value.astype(BF)
                rs_send(s, i, way, 0)
        else:
            rs_wait(s, hz - 1)
            settle(s, part[s, z] + (z_recv[s, 0, hz - 1].astype(F32) + z_recv[s, 1, hz - 1].astype(F32)))

    def rs_short(s, i):
        if i == 0:
            for way in range(2):
                z_send[s, way, 1] = part[s, chunk_at(signs[way] * 3)].astype(BF)
                rs_send(s, 1, way, 0)
            rs_first(s, 1)
            for way in range(2):
                z_send[s, way, 2] = part[s, chunk_at(signs[way])].astype(BF)
                rs_send(s, 2, way, 0)
        elif i == 1:
            rs_wait(s, 1)
            rs_wait(s, 0)
            for way in range(2):
                value = part[s, chunk_at(signs[way] * 2)] + z_recv[s, way, 1].astype(F32)
                z_send[s, way, 3] = with_half(s, way, value).astype(BF)
                rs_send(s, 3, way, 1)
        else:
            rs_wait(s, 2)
            rs_wait(s, 3)
            total = part[s, z]
            for k in (2, 3):
                total = total + (z_recv[s, 0, k].astype(F32) + z_recv[s, 1, k].astype(F32))
            settle(s, total)

    def ag_block(s, way, i):
        block = (s // 2, s % 2, chunk_at(-signs[way] * i))
        return block + (pl.ds(16 * way, 16),) if i == hz else block

    def ag_send(s, way, i, far):
        block = wide.at[ag_block(s, way, i - 1 - far) + ((pl.ds(16 * way, 16),) if i == hz else ())]
        launch(remote(block, block, send_sem.at[4], a_rsem.at[s, i - 1], hop[far][way]))

    def ag_wait(s, i):
        a, t = s // 2, s % 2
        both = wide.at[a, t, pl.ds(0, 2)] if i < hz else wide.at[a, t, 0]
        arrived(both, a_rsem.at[s, i - 1])

    def ag_chain(s, i):
        if i > 0:
            ag_wait(s, i)
        if i < hz:
            for way in range(2):
                ag_send(s, way, i + 1, 0)

    def ag_short(s, i):
        if i == 0:
            for way in range(2):
                ag_send(s, way, 2, 1)
            for way in range(2):
                ag_send(s, way, 1, 0)
        elif i == 1:
            ag_wait(s, 2)
            for way in range(2):
                ag_send(s, way, 3, 0)
            for way in range(2):
                ag_send(s, way, 4, 1)
        else:
            for k in (1, 3, 4):
                ag_wait(s, k)

    def rs_step(s, i):
        (rs_short if s in SHORT_SUMS else rs_chain)(s, i)

    def ag_step(s, i):
        (ag_short if s in SHORT_GATHERS else ag_chain)(s, i)

    near = hz - 2

    def span(early):
        return (-near, 2 * near + 1) if early else (near + 1, nz - 2 * near - 1)

    def product(s, early):
        a, t = s // 2, s % 2
        low, count = span(early)
        chunks = [chunk_at(low + d) for d in range(count)]
        rows = jnp.concatenate([wide[a, t, k] for k in chunks], axis=0)
        each = rows.shape[0] // len(chunks)
        for which, ref in ((o, oth_sum), (c, own_sum)):
            step = 256 if half % 256 == 0 else half
            for k in range(0, half, step):
                if a == 0:
                    value = contract(rows, wout[which, :, k:k + step], 1, 0)
                else:
                    value = contract(rows, win[which, k:k + step, :], 1, 1)
                for i, chunk in enumerate(chunks):
                    ref[s, pl.ds(chunk * per, per), :, k:k + step] = value[i * each:(i + 1) * each].reshape(per, 16, step)
            if ref is oth_sum:
                for chunk in chunks:
                    there = pl.ds(chunk * per, per)
                    launch(remote(
                        oth_sum.at[s, there], sib_sum.at[s, there], send_sem.at[7 + s], sib_rsem.at[s, 0 if early else 1], sibling
                    ))

    mine = y * n + x
    per = n * n // nz

    def spread(s, early):
        low, count = span(early)
        count = count * per
        arrived(sib_sum.at[s, pl.ds(0, count)], sib_rsem.at[s, 0 if early else 1])
        for i in range(count):
            k = lax.rem(mine + i, count)
            b = chunk_at(low + k // per) * per + lax.rem(k, per)

            @pl.when(b != mine)
            def _():
                out_send[s, b] = (own_sum[s, b] + sib_sum[s, b]).astype(BF)
                remote(
                    out_send.at[s, b], out_recv.at[s, mine], send_sem.at[5], out_rsem.at[s], at(lax.rem(b, n), b // n, z, c)
                ).start()

    results = (out_ref, gin_ref)

    def finish(s):
        a, t = s // 2, s % 2
        out_recv[s, mine] = jnp.zeros(out_recv.shape[2:], BF)
        value = own_sum[s, mine] + sib_sum[s, mine]
        arrived(out_recv.at[s, pl.ds(0, n * n - 1)], out_rsem.at[s])
        for k in range(n * n):
            value = value + out_recv[s, k].astype(F32)
        value = value.astype(BF)

        @pl.when(c != t)
        def _():
            fin_send[a] = value
            remote(fin_send.at[a], fin_recv.at[a], send_sem.at[6], fin_rsem.at[a], sibling).start()

        @pl.when(c == t)
        def _():
            cols = slice(t * half, (t + 1) * half)
            results[a][:, cols] = value

    def collect(a):
        arrived(fin_recv.at[a], fin_rsem.at[a])
        for t in range(2):
            @pl.when(c == t)
            def _():
                cols = slice((1 - t) * half, (2 - t) * half)
                results[a][:, cols] = fin_recv[a]

    def grad_w_out(h):
        cols = jnp.concatenate([rows_of(1, h, t) for t in range(2)], axis=0)
        step = 256 if width % 256 == 0 else width
        for k in range(0, width, step):
            left_rows = wide[0, :, :, :, k:k + step].reshape(-1, step)
            gw_out[h, k:k + step, :] = (contract(left_rows, cols, 0, 0) * factor).astype(BF)

    def grad_w_in(h):
        cols = wide[1].reshape(-1, width)
        step = 256 if half % 256 == 0 else half
        rows = jnp.concatenate([rows_of(0, h, t) for t in range(2)], axis=0)
        for k in range(0, half, step):
            gw_in[h, k:k + step, :] = (contract(rows[:, k:k + step], cols, 0, 0) * factor).astype(BF)

    def weights(a):
        arrived((win, wout)[a], w_sem.at[a])

    steps = {
        "s1": s1, "s2": s2, "s3": s3, "s4": s4, "weights": weights, "partial": partial, "rs_step": rs_step, "ag_step": ag_step,
        "product": product, "spread": spread, "finish": finish, "collect": collect, "drain": drain,
        "grad_w_out": grad_w_out, "grad_w_in": grad_w_in,
    }
    for step, *place in SCHEDULE:
        steps[step](*place)


def hand_over(out, gin, gw_in, gw_out, out_to, gin_to, gw_in_to, gw_out_to, sem):
    half = gw_in.shape[1]
    parts = 4
    step = half // parts
    copies = []
    for h in range(2):
        for p in range(parts):
            k = len(copies)
            copies.append(pltpu.make_async_copy(
                gw_in.at[h, pl.ds(p * step, step)], gw_in_to.at[pl.ds(h * half + p * step, step), :], sem.at[k]
            ))
            copies.append(pltpu.make_async_copy(
                gw_out.at[h, pl.ds(p * step, step)], gw_out_to.at[pl.ds(p * step, step), pl.ds(h * half, half)], sem.at[k + 1]
            ))
    copies.append(pltpu.make_async_copy(out, out_to, sem.at[len(copies)]))
    copies.append(pltpu.make_async_copy(gin, gin_to, sem.at[len(copies)]))
    for copy in copies:
        copy.start()
    for copy in copies:
        copy.wait()


def shards(n, nz, inputs, w_in, w_out, grad_out):
    rows, wide_cols = inputs.shape
    half = wide_cols // 2
    quarter = half // 2
    width = w_in.shape[1]
    tokens = 2 * n * n * rows
    chunk = n * n * rows // nz
    any_spec = pl.BlockSpec(memory_space=pl.ANY)
    vmem_spec = pl.BlockSpec(memory_space=pltpu.VMEM)
    dma = pltpu.SemaphoreType.DMA
    hz = nz // 2
    scratch = [
        pltpu.VMEM((2, 2, 2, 2, n, n, rows, quarter), BF),
        pltpu.VMEM((2, half, width), BF),
        pltpu.VMEM((2, width, half), BF),
        pltpu.VMEM((4, nz, chunk, width), F32),
        pltpu.VMEM((4, 2, hz, chunk, width), BF),
        pltpu.VMEM((4, 2, hz, chunk, width), BF),
        pltpu.VMEM((2, chunk, width), F32),
        pltpu.VMEM((2, 2, nz, chunk, width), BF),
        pltpu.VMEM((4, n * n, rows, half), F32),
        pltpu.VMEM((4, n * n, rows, half), F32),
        pltpu.VMEM((4, n * n, rows, half), F32),
        pltpu.VMEM((4, n * n, rows, half), BF),
        pltpu.VMEM((4, n * n, rows, half), BF),
        pltpu.VMEM((2, rows, half), BF),
        pltpu.VMEM((2, rows, half), BF),
        pltpu.VMEM((2, 2, 2, rows, quarter), BF),
        dma((2,)), dma((2,)), dma((2, 2, 2)), dma((2, 2, 2, n - 1)), dma((2, 2)), dma((4, hz)), dma((4, hz)),
        dma((4, 2)), dma((4,)), dma((2,)), dma((11,)),
    ]
    results = pl.pallas_call(
        functools.partial(body, n, nz, 1.0 / tokens ** 0.5),
        name="ffn",
        out_shape=(
            pltpu.VMEM(inputs.shape, BF),
            pltpu.VMEM(inputs.shape, BF),
            pltpu.VMEM((2, half, width), BF),
            pltpu.VMEM((2, width, half), BF),
        ),
        in_specs=[any_spec] * 4,
        out_specs=(vmem_spec,) * 4,
        scratch_shapes=scratch,
        compiler_params=pltpu.CompilerParams(
            collective_id=0, has_side_effects=True, vmem_limit_bytes=48 * 2 ** 20
        ),
        cost_estimate=pl.CostEstimate(
            flops=12 * tokens * wide_cols * width, bytes_accessed=8 * wide_cols * width, transcendentals=0
        ),
    )(*(pltpu.with_memory_space_constraint(r, pltpu.HBM) for r in (inputs, w_in, w_out, grad_out)))
    return pl.pallas_call(
        hand_over,
        name="hand_over",
        out_shape=tuple(jax.ShapeDtypeStruct(a.shape, BF) for a in (inputs, inputs, w_in, w_out)),
        in_specs=[vmem_spec] * 4,
        out_specs=[any_spec] * 4,
        scratch_shapes=[dma((18,))],
        compiler_params=pltpu.CompilerParams(vmem_limit_bytes=4 * 2 ** 20),
    )(*(pltpu.with_memory_space_constraint(r, pltpu.VMEM) for r in results))


def solution(mesh):
    n, nz = mesh.shape["row"], mesh.shape["col"]
    in_specs = (
        P(("row", "depth"), "col"),
        P("col", ("row", "depth")),
        P(("row", "depth"), "col"),
        P(("row", "depth"), "col"),
    )
    out_specs = (
        P(("row", "depth"), "col"),
        P(("row", "depth"), "col"),
        P("col", ("row", "depth")),
        P(("row", "depth"), "col"),
    )
    return jax.shard_map(
        functools.partial(shards, n, nz), mesh=mesh, in_specs=in_specs, out_specs=out_specs, check_vma=False
    )
```

```python
import functools

import jax
import jax.numpy as jnp
from jax import lax
from jax.experimental import pallas as pl
from jax.experimental.pallas import tpu as pltpu
from jax.sharding import PartitionSpec as P

MESH = pl.DeviceIdType.MESH
BF = jnp.bfloat16
F32 = jnp.float32


SHORT_SUMS = (0,)
SHORT_GATHERS = ()

SCHEDULE = (
    ("s1", 0), ("s1", 1), ("s2", 0, 1), ("s2", 0, 0), ("s2", 1, 1), ("s2", 1, 0), ("s3", 0, 1), ("weights", 0),
    ("partial", 0, 1, False), ("s4", 0, 1), ("partial", 0, 1, True), ("s3", 0, 0), ("rs_step", 1, 0),
    ("partial", 0, 0, False), ("s4", 0, 0), ("partial", 0, 0, True), ("rs_step", 0, 0), ("s3", 1, 1), ("weights", 1),
    ("partial", 1, 1, False), ("rs_step", 1, 1), ("s4", 1, 1), ("partial", 1, 1, True), ("rs_step", 3, 0),
    ("s3", 1, 0), ("partial", 1, 0, False), ("s4", 1, 0), ("partial", 1, 0, True), ("rs_step", 2, 0),
    ("rs_step", 0, 1), ("rs_step", 1, 2), ("rs_step", 3, 1), ("rs_step", 2, 1), ("rs_step", 0, 2), ("ag_step", 0, 0),
    ("rs_step", 1, 3), ("rs_step", 3, 2), ("rs_step", 2, 2), ("ag_step", 0, 1), ("rs_step", 1, 4), ("ag_step", 1, 0),
    ("rs_step", 3, 3), ("rs_step", 2, 3), ("ag_step", 0, 2), ("product", 0, True), ("ag_step", 1, 1),
    ("rs_step", 3, 4), ("ag_step", 3, 0), ("spread", 0, True), ("rs_step", 2, 4), ("ag_step", 2, 0),
    ("ag_step", 0, 3), ("ag_step", 1, 2), ("product", 1, True), ("ag_step", 3, 1), ("ag_step", 2, 1),
    ("spread", 1, True), ("ag_step", 0, 4), ("product", 0, False), ("ag_step", 1, 3), ("ag_step", 3, 2),
    ("product", 3, True), ("spread", 0, False), ("ag_step", 2, 2), ("product", 2, True), ("ag_step", 1, 4),
    ("product", 1, False), ("spread", 3, True), ("grad_w_out", 0), ("ag_step", 3, 3), ("spread", 1, False),
    ("ag_step", 2, 3), ("spread", 2, True), ("finish", 0), ("grad_w_out", 1), ("ag_step", 3, 4),
    ("product", 3, False), ("ag_step", 2, 4), ("product", 2, False), ("grad_w_in", 0), ("spread", 3, False),
    ("spread", 2, False), ("finish", 1), ("grad_w_in", 1), ("collect", 0), ("finish", 3), ("finish", 2),
    ("collect", 1), ("drain",),
)


def gelu_parts(hidden):
    inner = 0.7978845608 * (hidden + 0.044715 * hidden * hidden * hidden)
    tangent = jnp.tanh(inner)
    value = 0.5 * hidden * (1.0 + tangent)
    slope = 0.5 * (1.0 + tangent) + 0.5 * hidden * (1.0 - tangent * tangent) * 0.7978845608 * (
        1.0 + 3.0 * 0.044715 * hidden * hidden
    )
    return (value, slope)


def contract(left, right, left_dim, right_dim):
    return lax.dot_general(
        left, right, (((left_dim,), (right_dim,)), ((), ())), preferred_element_type=F32
    )


def body(
    n, nz, factor,
    x_hbm, win_hbm, wout_hbm, g_hbm,
    out_ref, gin_ref, gw_in, gw_out,
    acts, win, wout, part, z_send, z_recv, slope_ref, wide,
    own_sum, oth_sum, sib_sum, out_send, out_recv, fin_send, fin_recv,
    own_rows,
    w_sem, x_sem, s1_rsem, s2_rsem, sp_rsem, z_rsem, a_rsem, sib_rsem, out_rsem, fin_rsem, send_sem,
):
    y = lax.axis_index("row")
    z = lax.axis_index("col")
    depth = lax.axis_index("depth")
    x, c = depth // 2, lax.rem(depth, 2)
    o = 1 - c
    half = win.shape[1]
    quarter = half // 2
    width = win.shape[2]
    wmid = width // 2

    def at(xx, yy, zz, cc):
        return (lax.rem(yy, n), lax.rem(zz, nz), lax.rem(xx, n) * 2 + cc)

    sibling = at(x, y, z, o)
    hop = [[at(x, y, z + d, c) for d in (1, nz - 1)], [at(x, y, z + d, c) for d in (2, nz - 2)]]

    places = ((x, y), (y, x))

    def line(q, axis, d):
        return at(x + d, y, z, c) if q == axis else at(x, y + d, z, c)

    def back(q, d):
        return lax.rem(q + (n - d), n)

    def ahead(q, d):
        return lax.rem(q + d, n)

    def remote(src, dst, ssem, rsem, device):
        return pltpu.make_async_remote_copy(
            src_ref=src, dst_ref=dst, send_sem=ssem, recv_sem=rsem, device_id=device, device_id_type=MESH
        )

    x_copies, w_copies = [], []
    for a, src in enumerate((x_hbm, g_hbm)):
        for h in range(2):
            for q in range(2):
                cols = pl.ds(h * half + q * quarter, quarter)
                x_copies.append(pltpu.make_async_copy(src.at[:, cols], own_rows.at[a, h, q], x_sem.at[a]))
    for h in range(2):
        w_copies.append(pltpu.make_async_copy(win_hbm.at[pl.ds(h * half, half), :], win.at[h], w_sem.at[0]))
        w_copies.append(pltpu.make_async_copy(wout_hbm.at[:, pl.ds(h * half, half)], wout.at[h], w_sem.at[1]))
    for copy in x_copies:
        copy.start()

    barrier = pltpu.get_barrier_semaphore()
    partners = [sibling]
    for d in sorted({1, 2, nz - 2, nz - 1}):
        partners.append(at(x, y, z + d, c))
    for d in range(1, n):
        for cc in range(2):
            partners.append(at(x + d, y, z, cc))
            partners.append(at(x, y + d, z, cc))
        for e in range(1, n):
            partners.append(at(x + d, y + e, z, c))
    for partner in partners:
        pl.semaphore_signal(barrier, inc=1, device_id=partner, device_id_type=MESH)
    pl.semaphore_wait(barrier, len(partners))

    def launch(copy):
        copy.start()
        return copy

    def arrived(ref, sem):
        pltpu.make_async_copy(ref, ref, sem).wait()

    def drain():
        blocks = own_sum
        for k, ref in enumerate((
            blocks.at[0, pl.ds(0, 2 * n - 1)],
            blocks.at[pl.ds(0, 2), pl.ds(0, n * (n - 1))],
            blocks.at[pl.ds(0, 2)],
            part.at[pl.ds(0, 2), pl.ds(0, nz - 1)],
            part.at[pl.ds(0, 2), pl.ds(0, nz - 1)],
            blocks.at[pl.ds(0, 2), pl.ds(0, n * n - 1)],
            fin_send,
            blocks.at[0], blocks.at[1], blocks.at[2], blocks.at[3],
        )):
            arrived(ref, send_sem.at[k])

    def s1(a):
        arrived(own_rows.at[a], x_sem.at[a])
        for d in (2, 1, 3):
            if d >= n:
                continue
            for h in range(2):
                for q in range(2):
                    first, second = places[q]
                    there = at(x + d, y, z, h) if q == 0 else at(x, y + d, z, h)
                    launch(remote(
                        own_rows.at[a, h, q], acts.at[a, h, q, c, second, first], send_sem.at[0], s1_rsem.at[a, c, q], there
                    ))
        for q in range(2):
            first, second = places[q]
            launch(remote(
                own_rows.at[a, o, q], acts.at[a, o, q, c, second, first], send_sem.at[0], s1_rsem.at[a, c, q], sibling
            ))
            launch(pltpu.make_async_copy(
                own_rows.at[a, c, q], acts.at[a, c, q, c, second, first], s1_rsem.at[a, c, q]
            ))
        if a == 0:
            for copy in w_copies:
                copy.start()

    def s2(a, t):
        for q in range(2):
            row = acts.at[a, c, q, t, places[q][1]]
            arrived(row, s1_rsem.at[a, t, q])
            for d in (2, 1, 3):
                if d < n:
                    launch(remote(row, row, send_sem.at[1], s2_rsem.at[a, t, q, d - 1], line(q, 1, d)))
            launch(remote(row, row, send_sem.at[2], sp_rsem.at[a, t], sibling))

    def s3(a, t):
        for d in (1, 3, 2):
            if d >= n:
                continue
            for q in range(2):
                row = acts.at[a, c, q, t, back(places[q][1], d)]
                arrived(row, s2_rsem.at[a, t, q, d - 1])
                launch(remote(row, row, send_sem.at[2], sp_rsem.at[a, t], sibling))

    def s4(a, t):
        arrived(acts.at[a, o, :, t], sp_rsem.at[a, t])

    def rows_of(a, h, t):
        across = [acts[a, h, 0, t].reshape(n * n * 16, quarter)]
        across.append(jnp.concatenate([acts[a, h, 1, t, i, j] for j in range(n) for i in range(n)], axis=0))
        return jnp.concatenate(across, axis=1)

    def partial(a, t, theirs):
        s = 2 * a + t
        h = o if theirs else c
        rows = rows_of(a, h, t)
        step = 256 if width % 256 == 0 else width
        for k in range(0, width, step):
            if a == 0:
                value = contract(rows, win[h, :, k:k + step], 1, 0)
            else:
                value = contract(rows, wout[h, k:k + step, :], 1, 1)
            value = value.reshape(nz, -1, step)
            if theirs:
                value = value + part[s, :, :, k:k + step]
            part[s, :, :, k:k + step] = value

    hz = nz // 2
    signs = (1, -1)

    def chunk_at(d):
        return lax.rem(z + (d + nz), nz)

    def rs_send(s, i, way, far):
        cols = (slice(None), pl.ds(0, wmid)) if i == 0 else ()
        ref = (s, way, i) + cols
        launch(remote(z_send.at[ref], z_recv.at[ref], send_sem.at[3], z_rsem.at[s, i], hop[far][way]))

    def rs_wait(s, i):
        ref = z_recv.at[s, :, 0, :, pl.ds(0, wmid)] if i == 0 else z_recv.at[s, :, i]
        arrived(ref, z_rsem.at[s, i])

    def rs_first(s, far):
        for way in range(2):
            z_send[s, way, 0, :, :wmid] = part[s, chunk_at(hz), :, way * wmid:(way + 1) * wmid].astype(BF)
            rs_send(s, 0, way, far)

    def with_half(s, way, value):
        half_in = z_recv[s, way, 0, :, :wmid].astype(F32)
        if way == 0:
            return jnp.concatenate([value[:, :wmid] + half_in, value[:, wmid:]], axis=1)
        return jnp.concatenate([value[:, :wmid], value[:, wmid:] + half_in], axis=1)

    def settle(s, total):
        t = s % 2
        if s < 2:
            value, slope = gelu_parts(total)
            slope_ref[t] = slope
            wide[0, t, z] = value.astype(BF)
        else:
            wide[1, t, z] = (total * slope_ref[t]).astype(BF)

    def rs_chain(s, i):
        if i == 0:
            rs_first(s, 0)
        elif i < hz:
            rs_wait(s, i - 1)
            for way in range(2):
                value = part[s, chunk_at(signs[way] * (hz - i))]
                if i == 1:
                    value = with_half(s, way, value)
                else:
                    value = value + z_recv[s, way, i - 1].astype(F32)
                z_send[s, way, i] = value.astype(BF)
                rs_send(s, i, way, 0)
        else:
            rs_wait(s, hz - 1)
            settle(s, part[s, z] + (z_recv[s, 0, hz - 1].astype(F32) + z_recv[s, 1, hz - 1].astype(F32)))

    def rs_short(s, i):
        if i == 0:
            for way in range(2):
                z_send[s, way, 1] = part[s, chunk_at(signs[way] * 3)].astype(BF)
                rs_send(s, 1, way, 0)
            rs_first(s, 1)
            for way in range(2):
                z_send[s, way, 2] = part[s, chunk_at(signs[way])].astype(BF)
                rs_send(s, 2, way, 0)
        elif i == 1:
            rs_wait(s, 1)
            rs_wait(s, 0)
            for way in range(2):
                value = part[s, chunk_at(signs[way] * 2)] + z_recv[s, way, 1].astype(F32)
                z_send[s, way, 3] = with_half(s, way, value).astype(BF)
                rs_send(s, 3, way, 1)
        else:
            rs_wait(s, 2)
            rs_wait(s, 3)
            total = part[s, z]
            for k in (2, 3):
                total = total + (z_recv[s, 0, k].astype(F32) + z_recv[s, 1, k].astype(F32))
            settle(s, total)

    def ag_block(s, way, i):
        block = (s // 2, s % 2, chunk_at(-signs[way] * i))
        return block + (pl.ds(16 * way, 16),) if i == hz else block

    def ag_send(s, way, i, far):
        block = wide.at[ag_block(s, way, i - 1 - far) + ((pl.ds(16 * way, 16),) if i == hz else ())]
        launch(remote(block, block, send_sem.at[4], a_rsem.at[s, i - 1], hop[far][way]))

    def ag_wait(s, i):
        a, t = s // 2, s % 2
        both = wide.at[a, t, pl.ds(0, 2)] if i < hz else wide.at[a, t, 0]
        arrived(both, a_rsem.at[s, i - 1])

    def ag_chain(s, i):
        if i > 0:
            ag_wait(s, i)
        if i < hz:
            for way in range(2):
                ag_send(s, way, i + 1, 0)

    def ag_short(s, i):
        if i == 0:
            for way in range(2):
                ag_send(s, way, 2, 1)
            for way in range(2):
                ag_send(s, way, 1, 0)
        elif i == 1:
            ag_wait(s, 2)
            for way in range(2):
                ag_send(s, way, 3, 0)
            for way in range(2):
                ag_send(s, way, 4, 1)
        else:
            for k in (1, 3, 4):
                ag_wait(s, k)

    def rs_step(s, i):
        (rs_short if s in SHORT_SUMS else rs_chain)(s, i)

    def ag_step(s, i):
        (ag_short if s in SHORT_GATHERS else ag_chain)(s, i)

    near = hz - 2

    def span(early):
        return (-near, 2 * near + 1) if early else (near + 1, nz - 2 * near - 1)

    def product(s, early):
        a, t = s // 2, s % 2
        low, count = span(early)
        chunks = [chunk_at(low + d) for d in range(count)]
        rows = jnp.concatenate([wide[a, t, k] for k in chunks], axis=0)
        each = rows.shape[0] // len(chunks)
        for which, ref in ((o, oth_sum), (c, own_sum)):
            step = 256 if half % 256 == 0 else half
            for k in range(0, half, step):
                if a == 0:
                    value = contract(rows, wout[which, :, k:k + step], 1, 0)
                else:
                    value = contract(rows, win[which, k:k + step, :], 1, 1)
                for i, chunk in enumerate(chunks):
                    ref[s, pl.ds(chunk * per, per), :, k:k + step] = value[i * each:(i + 1) * each].reshape(per, 16, step)
            if ref is oth_sum:
                for chunk in chunks:
                    there = pl.ds(chunk * per, per)
                    launch(remote(
                        oth_sum.at[s, there], sib_sum.at[s, there], send_sem.at[7 + s], sib_rsem.at[s, 0 if early else 1], sibling
                    ))

    mine = y * n + x
    per = n * n // nz

    def spread(s, early):
        low, count = span(early)
        count = count * per
        arrived(sib_sum.at[s, pl.ds(0, count)], sib_rsem.at[s, 0 if early else 1])
        for i in range(count):
            k = lax.rem(mine + i, count)
            b = chunk_at(low + k // per) * per + lax.rem(k, per)

            @pl.when(b != mine)
            def _():
                out_send[s, b] = (own_sum[s, b] + sib_sum[s, b]).astype(BF)
                remote(
                    out_send.at[s, b], out_recv.at[s, mine], send_sem.at[5], out_rsem.at[s], at(lax.rem(b, n), b // n, z, c)
                ).start()

    results = (out_ref, gin_ref)

    def finish(s):
        a, t = s // 2, s % 2
        out_recv[s, mine] = jnp.zeros(out_recv.shape[2:], BF)
        value = own_sum[s, mine] + sib_sum[s, mine]
        arrived(out_recv.at[s, pl.ds(0, n * n - 1)], out_rsem.at[s])
        for k in range(n * n):
            value = value + out_recv[s, k].astype(F32)
        value = value.astype(BF)

        @pl.when(c != t)
        def _():
            fin_send[a] = value
            remote(fin_send.at[a], fin_recv.at[a], send_sem.at[6], fin_rsem.at[a], sibling).start()

        @pl.when(c == t)
        def _():
            cols = slice(t * half, (t + 1) * half)
            results[a][:, cols] = value

    def collect(a):
        arrived(fin_recv.at[a], fin_rsem.at[a])
        for t in range(2):
            @pl.when(c == t)
            def _():
                cols = slice((1 - t) * half, (2 - t) * half)
                results[a][:, cols] = fin_recv[a]

    def grad_w_out(h):
        cols = jnp.concatenate([rows_of(1, h, t) for t in range(2)], axis=0)
        step = 256 if width % 256 == 0 else width
        for k in range(0, width, step):
            left_rows = wide[0, :, :, :, k:k + step].reshape(-1, step)
            gw_out[h, k:k + step, :] = (contract(left_rows, cols, 0, 0) * factor).astype(BF)

    def grad_w_in(h):
        cols = wide[1].reshape(-1, width)
        step = 256 if half % 256 == 0 else half
        rows = jnp.concatenate([rows_of(0, h, t) for t in range(2)], axis=0)
        for k in range(0, half, step):
            gw_in[h, k:k + step, :] = (contract(rows[:, k:k + step], cols, 0, 0) * factor).astype(BF)

    def weights(a):
        arrived((win, wout)[a], w_sem.at[a])

    steps = {
        "s1": s1, "s2": s2, "s3": s3, "s4": s4, "weights": weights, "partial": partial, "rs_step": rs_step, "ag_step": ag_step,
        "product": product, "spread": spread, "finish": finish, "collect": collect, "drain": drain,
        "grad_w_out": grad_w_out, "grad_w_in": grad_w_in,
    }
    for step, *place in SCHEDULE:
        steps[step](*place)


def hand_over(out, gin, gw_in, gw_out, out_to, gin_to, gw_in_to, gw_out_to, sem):
    half = gw_in.shape[1]
    parts = 4
    step = half // parts
    copies = []
    for h in range(2):
        for p in range(parts):
            k = len(copies)
            copies.append(pltpu.make_async_copy(
                gw_in.at[h, pl.ds(p * step, step)], gw_in_to.at[pl.ds(h * half + p * step, step), :], sem.at[k]
            ))
            copies.append(pltpu.make_async_copy(
                gw_out.at[h, pl.ds(p * step, step)], gw_out_to.at[pl.ds(p * step, step), pl.ds(h * half, half)], sem.at[k + 1]
            ))
    copies.append(pltpu.make_async_copy(out, out_to, sem.at[len(copies)]))
    copies.append(pltpu.make_async_copy(gin, gin_to, sem.at[len(copies)]))
    for copy in copies:
        copy.start()
    for copy in copies:
        copy.wait()


def shards(n, nz, inputs, w_in, w_out, grad_out):
    rows, wide_cols = inputs.shape
    half = wide_cols // 2
    quarter = half // 2
    width = w_in.shape[1]
    tokens = 2 * n * n * rows
    chunk = n * n * rows // nz
    any_spec = pl.BlockSpec(memory_space=pl.ANY)
    vmem_spec = pl.BlockSpec(memory_space=pltpu.VMEM)
    dma = pltpu.SemaphoreType.DMA
    hz = nz // 2
    scratch = [
        pltpu.VMEM((2, 2, 2, 2, n, n, rows, quarter), BF),
        pltpu.VMEM((2, half, width), BF),
        pltpu.VMEM((2, width, half), BF),
        pltpu.VMEM((4, nz, chunk, width), F32),
        pltpu.VMEM((4, 2, hz, chunk, width), BF),
        pltpu.VMEM((4, 2, hz, chunk, width), BF),
        pltpu.VMEM((2, chunk, width), F32),
        pltpu.VMEM((2, 2, nz, chunk, width), BF),
        pltpu.VMEM((4, n * n, rows, half), F32),
        pltpu.VMEM((4, n * n, rows, half), F32),
        pltpu.VMEM((4, n * n, rows, half), F32),
        pltpu.VMEM((4, n * n, rows, half), BF),
        pltpu.VMEM((4, n * n, rows, half), BF),
        pltpu.VMEM((2, rows, half), BF),
        pltpu.VMEM((2, rows, half), BF),
        pltpu.VMEM((2, 2, 2, rows, quarter), BF),
        dma((2,)), dma((2,)), dma((2, 2, 2)), dma((2, 2, 2, n - 1)), dma((2, 2)), dma((4, hz)), dma((4, hz)),
        dma((4, 2)), dma((4,)), dma((2,)), dma((11,)),
    ]
    results = pl.pallas_call(
        functools.partial(body, n, nz, 1.0 / tokens ** 0.5),
        name="ffn",
        out_shape=(
            pltpu.VMEM(inputs.shape, BF),
            pltpu.VMEM(inputs.shape, BF),
            pltpu.VMEM((2, half, width), BF),
            pltpu.VMEM((2, width, half), BF),
        ),
        in_specs=[any_spec] * 4,
        out_specs=(vmem_spec,) * 4,
        scratch_shapes=scratch,
        compiler_params=pltpu.CompilerParams(
            collective_id=0, has_side_effects=True, vmem_limit_bytes=48 * 2 ** 20
        ),
        cost_estimate=pl.CostEstimate(
            flops=12 * tokens * wide_cols * width, bytes_accessed=8 * wide_cols * width, transcendentals=0
        ),
    )(*(pltpu.with_memory_space_constraint(r, pltpu.HBM) for r in (inputs, w_in, w_out, grad_out)))
    return pl.pallas_call(
        hand_over,
        name="hand_over",
        out_shape=tuple(jax.ShapeDtypeStruct(a.shape, BF) for a in (inputs, inputs, w_in, w_out)),
        in_specs=[vmem_spec] * 4,
        out_specs=[any_spec] * 4,
        scratch_shapes=[dma((18,))],
        compiler_params=pltpu.CompilerParams(vmem_limit_bytes=4 * 2 ** 20),
    )(*(pltpu.with_memory_space_constraint(r, pltpu.VMEM) for r in results))


def solution(mesh):
    n, nz = mesh.shape["row"], mesh.shape["col"]
    in_specs = (
        P(("row", "depth"), "col"),
        P("col", ("row", "depth")),
        P(("row", "depth"), "col"),
        P(("row", "depth"), "col"),
    )
    out_specs = (
        P(("row", "depth"), "col"),
        P(("row", "depth"), "col"),
        P("col", ("row", "depth")),
        P(("row", "depth"), "col"),
    )
    return jax.shard_map(
        functools.partial(shards, n, nz), mesh=mesh, in_specs=in_specs, out_specs=out_specs, check_vma=False
    )
```
